256 devices in a mesh: leaf: 128 (over y, z_lo, x, core), band: 2 (over z_hi).
Axes of the slice: x: 4, y: 4, z: 8 (z_hi: 2, z_lo: 4; z = z_hi * 4 + z_lo), core: 2. Of those that a mesh axis runs over, the one named last changes fastest.
Arguments:
- weights: float32 [2, 1048576, 128], P('band', 'leaf'), may hold values from -6 to 6
- rates: float32 [2, 4, 2, 1048576], P('band', None, None, 'leaf'), may hold values from -16 to 16
- translate: float32 [4, 2, 64, 64], replicated, may hold values from -0.5 to 0.5
- evaluate: float32 [2, 2, 64, 64], P('band'), may hold values from -0.5 to 0.5
Outputs:
- image: float32 [1048576, 128], P(('leaf', 'band'))
The draws below stay inside these ranges and needn't reach their ends.
All inputs are finite; a program needn't handle non-finite values.
Results may differ from the reference program's by a relative error of at most 0.0003.
Values sent between devices are 32-bit elements; how exact they have to be, the bound alone decides.
No kernel may reach another device: no remote copies, remote signals or barrier semaphores. Data moves between devices by JAX's collectives and lax.ppermute only.
A program may use at most 128 MiB of HBM per device.

```python
import jax
import jax.numpy as jnp
from jax import lax

R = 64
PIX = 64
LEVELS = 4
BOX_DEV = 8192
BANDS = 2
BOXES = 1048576
N_LEAF = 128


def shard_levels(stream_key, shape, pieces, least, top_value):
    loudness, own = 1.0, jax.random.fold_in(stream_key, 6)
    for axis_at, parts in pieces:
        heights = jnp.exp(jax.random.uniform(jax.random.fold_in(own, axis_at), (parts,), jnp.float32, least / len(pieces), top_value / len(pieces)))
        loudness = loudness * jnp.repeat(heights, shape[axis_at] // parts).reshape([-1 if axis == axis_at else 1 for axis in range(len(shape))])
    return loudness


def bell_draw(key, dims, width, reach, shards=(), held_as=jnp.bfloat16):
    drawn = width * jax.random.normal(key, dims, jnp.float32)
    if shards:
        drawn = drawn * shard_levels(key, dims, shards, -0.22, 0.18)
    return jnp.clip(drawn, -reach, reach).astype(held_as)


def setup_inputs(seed: int = 0) -> dict:
    splits = jax.random.split(jax.random.key(seed), 5)
    return {
        "weights": bell_draw(splits[0], (BANDS, BOXES, 2 * R), 1.0, 6.0, ((0, 2), (1, 128)), jnp.float32),
        "rates": bell_draw(splits[1], (BANDS, LEVELS, 2, BOXES), 4.0, 16.0, ((0, 2), (3, 128)), jnp.float32),
        "translate": bell_draw(splits[2], (LEVELS, 2, R, R), (2 * R) ** -0.5, 0.5, (), jnp.float32),
        "evaluate": bell_draw(splits[3], (BANDS, 2, R, PIX), (2 * R) ** -0.5, 0.5, ((0, 2),), jnp.float32),
    }


HIGH = lax.Precision.HIGHEST


def cheb_nodes(node_count):
    ticks = jnp.arange(node_count).astype(jnp.float32)
    return 0.5 * (1.0 - jnp.cos(jnp.pi * (ticks + 0.5) / node_count))


def translate_rows(rows, linear_rate, square_rate, source_nodes, matrix):
    angle = linear_rate[:, :, None] * source_nodes + square_rate[:, :, None] * source_nodes * source_nodes
    cosine = jnp.cos(angle)
    sine = jnp.sin(angle)
    real_in = rows[None, :, 0, :]
    imag_in = rows[None, :, 1, :]
    real_mod = cosine * real_in - sine * imag_in
    imag_mod = sine * real_in + cosine * imag_in
    real_out = jnp.einsum('chk,kj->chj', real_mod, matrix, precision=HIGH)
    imag_out = jnp.einsum('chk,kj->chj', imag_mod, matrix, precision=HIGH)
    return real_out, imag_out


def rotate_back(real_sum, imag_sum, linear_rate, square_rate, parent):
    angle = linear_rate[:, :, None] * parent + square_rate[:, :, None] * parent * parent
    cosine = jnp.cos(angle)
    sine = jnp.sin(angle)
    return jnp.stack([cosine * real_sum + sine * imag_sum, cosine * imag_sum - sine * real_sum], axis=2)


def reference(weights, rates, translate, evaluate):
    parent = cheb_nodes(R)
    half_rows = BOX_DEV // 2
    top = N_LEAF.bit_length() - 1
    total = jnp.zeros((N_LEAF * BOX_DEV, 2 * PIX), jnp.float32)
    for band_index in range(BANDS):
        state = weights[band_index].reshape(N_LEAF, 2, half_rows, 2, R)
        for level_index in range(LEVELS):
            bit_pos = top - 1 - level_index
            stride = 1 << bit_pos
            level_rates = rates[band_index, level_index].reshape(2, N_LEAF, 2, half_rows).transpose(1, 0, 2, 3)
            translate_pair = translate[level_index]

            def one_device(device, state=state, level_rates=level_rates, translate_pair=translate_pair, bit_pos=bit_pos, stride=stride):
                keep = (device >> bit_pos) & 1
                lower = device - keep * stride
                upper = lower + stride
                first_rows = state[lower, keep]
                second_rows = state[upper, keep]
                own_rates = level_rates[device]
                real_lo, imag_lo = translate_rows(first_rows, own_rates[0], own_rates[1], parent * 0.5, translate_pair[0])
                real_hi, imag_hi = translate_rows(second_rows, own_rates[0], own_rates[1], (1.0 + parent) * 0.5, translate_pair[1])
                return rotate_back(real_lo + real_hi, imag_lo + imag_hi, own_rates[0], own_rates[1], parent)

            state = lax.map(one_device, jnp.arange(N_LEAF, dtype=jnp.int32))
        flat = state.reshape(N_LEAF * BOX_DEV, 2, R)
        eval_real = evaluate[band_index, 0]
        eval_imag = evaluate[band_index, 1]
        real_img = jnp.dot(flat[:, 0], eval_real, precision=HIGH, preferred_element_type=jnp.float32) - jnp.dot(flat[:, 1], eval_imag, precision=HIGH, preferred_element_type=jnp.float32)
        imag_img = jnp.dot(flat[:, 0], eval_imag, precision=HIGH, preferred_element_type=jnp.float32) + jnp.dot(flat[:, 1], eval_real, precision=HIGH, preferred_element_type=jnp.float32)
        total = total + jnp.concatenate([real_img, imag_img], axis=1)
    return total
```

```python
import functools

import jax
import jax.numpy as jnp
import ml_dtypes
import numpy as np
from jax import lax
from jax.experimental import pallas as pl
from jax.experimental.pallas import tpu as pltpu
from jax.sharding import Mesh, PartitionSpec as P

BF = jnp.bfloat16
F32 = jnp.float32
LANES = 128
GROUP = 32
TILE = 16
MAGIC = 12582912.0


def split3(values):
    parts = []
    rest = values.astype(np.float64)
    for _ in range(3):
        part = rest.astype(ml_dtypes.bfloat16).astype(np.float64)
        parts.append(part)
        rest = rest - part
    return parts


def angle_rows(linear, square, offset):
    l1, l2, l3 = split3(linear)
    s1, s2, s3 = split3(square)
    zero = np.zeros_like(linear)
    return [l1, s1, l2, s2, l3, s3, l1, s1, l2, s2, l1, s1, offset, zero, zero, zero]


def angle_matrix(node_count):
    ticks = np.arange(node_count, dtype=np.float64)
    nodes = 0.5 * (1.0 - np.cos(np.pi * (ticks + 0.5) / node_count))
    both = np.concatenate([nodes, nodes])
    turn = 1.0 / (2.0 * np.pi)
    quarter = np.concatenate([np.zeros(node_count), np.full(node_count, -0.25)])
    zero = np.zeros(2 * node_count)
    low, high = both / 2, (1 + both) / 2
    own = np.concatenate(
        [
            np.stack(angle_rows(low * turn, low**2 * turn, quarter)),
            np.stack(angle_rows(high * turn, high**2 * turn, quarter)),
        ],
        axis=1,
    )
    undo = np.stack(angle_rows(-both * turn, -(both**2) * turn, zero))
    undo_quarter = np.stack(angle_rows(-both * turn, -(both**2) * turn, quarter))
    none = np.zeros_like(undo)
    level = np.concatenate(
        [own, np.concatenate([undo, none], 1), np.concatenate([none, undo], 1)], 0
    )
    last = np.concatenate(
        [np.concatenate([undo_quarter, none], 1), np.concatenate([none, undo_quarter], 1)], 0
    )
    return np.concatenate([level, last], 0).astype(ml_dtypes.bfloat16)


def cos_turns(t):
    r = t - ((t + MAGIC) - MAGIC)
    w = 0.25 - jnp.abs(r)
    z = w * w
    p = z * C4 + C3
    p = p * z + C2
    p = p * z + C1
    p = p * z + C0
    return p * w


def _fit():
    w = np.cos(np.pi * (np.arange(400) + 0.5) / 800) * 0.25
    z = w * w
    target = np.sin(2 * np.pi * w) / w
    basis = np.stack([z**n for n in range(5)], 1)
    return [float(c) for c in np.linalg.lstsq(basis * w[:, None], target * w, rcond=None)[0]]


C0, C1, C2, C3, C4 = _fit()


def kernel(rows, got_ref, mats_ref, angle_ref, out_ref, tiles, state_a, state_b):
    levels = 4
    row_id = lax.broadcasted_iota(jnp.int32, (TILE, rows), 0)
    even = row_id % 2 == 0

    def make_tiles(m, carry):
        for level in range(levels):
            for child in range(2):
                at = 2 * rows + level * 4 + child
                a = got_ref[m, at : at + 1, :]
                q = got_ref[m, at + 2 : at + 3, :]
                base = jnp.where(even, jnp.broadcast_to(a, even.shape), jnp.broadcast_to(q, even.shape))
                first = base.astype(BF).astype(F32)
                rest = base - first
                second = rest.astype(BF).astype(F32)
                third = rest - second
                tile = jnp.where(row_id < 6, first, jnp.where(row_id < 10, second, third))
                tile = jnp.where(row_id < 12, tile, jnp.where(row_id == 12, 1.0, 0.0))
                tiles[level, m, child] = tile.astype(BF)
        return carry

    lax.fori_loop(0, GROUP, make_tiles, 0)

    def angles(parts, matrix):
        return lax.dot_general(
            jnp.concatenate(parts, 0) if len(parts) > 1 else parts[0],
            matrix,
            (((0,), (0,)), ((), ())),
            preferred_element_type=F32,
        )

    def combine(sources, turns, stage):
        highs, lows = [], []
        for pairs, turn in zip(sources, turns):
            phase = cos_turns(turn)
            high, low = [], []
            for s in range(2):
                cs = phase[:, s * LANES : (s + 1) * LANES]
                for value in pairs[s]:
                    product = value * cs
                    top = product.astype(BF)
                    high.append(top)
                    low.append((product - top.astype(F32)).astype(BF))
            highs.append(jnp.concatenate(high, 1))
            lows.append(jnp.concatenate(low, 1))
        wide = jnp.dot(jnp.concatenate(highs, 0), mats_ref[stage], preferred_element_type=F32)
        narrow = jnp.dot(
            jnp.concatenate(lows, 0), mats_ref[stage, :, :LANES], preferred_element_type=F32
        )
        return wide[:, :LANES] + wide[:, LANES:] + narrow

    def swap(x):
        return pltpu.roll(x, LANES // 2, 1)

    def level_stage(level, read, write):
        bit = levels - 1 - level

        def body(m, carry):
            e = (m >> (bit + 1)) & 1
            k1 = m | (2 << bit)
            k0 = k1 - (2 << bit)
            x0, x1 = read(k0, e), read(k1, e)
            pairs = ((x0, swap(x0)), (x1, swap(x1)))
            turns = []
            for child in range(2):
                parts = [tiles[level, m, child]]
                if level:
                    parts += [tiles[level - 1, k0, e], tiles[level - 1, k1, e]]
                turns.append(angles(parts, angle_ref[: TILE * len(parts), :]))
            u = combine([pairs, pairs], turns, level)
            write[m, 0] = u[:rows]
            write[m, 1] = u[rows:]
            return carry

        lax.fori_loop(0, GROUP, body, 0, unroll=4)

    def read_got(k, e):
        return got_ref[k, pl.ds(pl.multiple_of(e * rows, rows), rows), :]

    level_stage(0, read_got, state_a)
    level_stage(1, lambda k, e: state_a[k, e], state_b)
    level_stage(2, lambda k, e: state_b[k, e], state_a)
    level_stage(3, lambda k, e: state_a[k, e], state_b)

    def last(i, carry):
        sources, turns = [], []
        for child in range(2):
            x0, x1 = state_b[2 * i, child], state_b[2 * i + 1, child]
            sources.append(((x0, swap(x0)), (x1, swap(x1))))
            parts = [tiles[levels - 1, 2 * i, child], tiles[levels - 1, 2 * i + 1, child]]
            turns.append(angles(parts, angle_ref[3 * TILE : 5 * TILE, :]))
        u = combine(sources, turns, levels)
        out_ref[2 * i] = u[:rows]
        out_ref[2 * i + 1] = u[rows:]
        return carry

    lax.fori_loop(0, GROUP // 2, last, 0, unroll=4)


def butterfly(got, mats, angle, rows):
    return pl.pallas_call(
        functools.partial(kernel, rows),
        out_shape=jax.ShapeDtypeStruct((GROUP, rows, LANES), F32),
        in_specs=[pl.BlockSpec(memory_space=pltpu.VMEM)] * 3,
        out_specs=pl.BlockSpec(memory_space=pltpu.VMEM),
        scratch_shapes=[
            pltpu.VMEM((4, GROUP, 2, TILE, rows), BF),
            pltpu.VMEM((GROUP, 2, rows, LANES), F32),
            pltpu.VMEM((GROUP, 2, rows, LANES), F32),
        ],
        compiler_params=pltpu.CompilerParams(vmem_limit_bytes=40 << 20),
    )(got, mats, angle)


def stage_matrices(translate, evaluate):
    zero = jnp.zeros_like(translate)
    levels = jnp.concatenate(
        [
            jnp.concatenate([translate, zero], -1),
            jnp.concatenate([-translate, zero], -1),
            jnp.concatenate([zero, translate], -1),
            jnp.concatenate([zero, translate], -1),
        ],
        axis=2,
    ).reshape(translate.shape[0], -1, LANES)
    er, ei = evaluate[:, 0], evaluate[:, 1]
    direct = jnp.concatenate([er, ei], -1)
    cross = jnp.concatenate([-ei, er], -1)
    last = jnp.concatenate([direct, -direct, cross, cross], axis=1).reshape(1, -1, LANES)
    whole = jnp.concatenate([levels, last], 0)
    high = lax.reduce_precision(whole, 8, 7)
    return jnp.concatenate([high, whole - high], -1).astype(BF)


def per_device(weights, rates, translate, evaluate):
    half = weights.shape[1] // 2
    rows = half // GROUP
    axes = ("y", "zl", "band")
    other = lax.ppermute(evaluate[0], "band", [(0, 1), (1, 0)])
    mine = lax.axis_index("band")
    both = jnp.stack(
        [jnp.where(mine == 0, evaluate[0], other), jnp.where(mine == 0, other, evaluate[0])]
    )
    mats = stage_matrices(translate, both)
    halves = weights[0].reshape(2, GROUP, rows, LANES)
    phase_rates = rates[0].reshape(16, GROUP, rows).transpose(1, 0, 2)
    message = jnp.concatenate([halves[0], halves[1], phase_rates], axis=1)
    got = lax.all_to_all(message, axes, 0, 0, tiled=True)
    angle = jnp.asarray(angle_matrix(LANES // 2))
    image = butterfly(got, mats, angle, rows)
    return lax.all_to_all(image, axes, 0, 0, tiled=True).reshape(half, LANES)


def solution(mesh):
    fine = Mesh(mesh.devices.reshape(4, 4, 4, 2, 2), ("y", "zl", "x", "core", "band"))
    leaf = ("y", "zl", "x", "core")
    return jax.shard_map(
        per_device,
        mesh=fine,
        in_specs=(P("band", leaf, None), P("band", None, None, leaf), P(), P("band", None, None, None)),
        out_specs=P((*leaf, "band"), None),
        check_vma=False,
    )
```

```python
import functools

import jax
import jax.numpy as jnp
import ml_dtypes
import numpy as np
from jax import lax
from jax.experimental import pallas as pl
from jax.experimental.pallas import tpu as pltpu
from jax.sharding import Mesh, PartitionSpec as P

BF = jnp.bfloat16
F32 = jnp.float32
LANES = 128
GROUP = 32
TILE = 16
MAGIC = 12582912.0
LEVELS = 4
HALF = 64
SLICE = 128
FIRST = 96
STEPS = (4, 16)
UNROLL = 2


def split3(values):
    parts = []
    rest = values.astype(np.float64)
    for _ in range(3):
        part = rest.astype(ml_dtypes.bfloat16).astype(np.float64)
        parts.append(part)
        rest = rest - part
    return parts


def angle_rows(linear, square, offset):
    l1, l2, l3 = split3(linear)
    s1, s2, s3 = split3(square)
    zero = np.zeros_like(linear)
    return [l1, s1, l2, s2, l3, s3, l1, s1, l2, s2, l1, s1, offset, zero, zero, zero]


def angle_matrix(node_count):
    ticks = np.arange(node_count, dtype=np.float64)
    nodes = 0.5 * (1.0 - np.cos(np.pi * (ticks + 0.5) / node_count))
    both = np.concatenate([nodes, nodes])
    turn = 1.0 / (2.0 * np.pi)
    quarter = np.concatenate([np.zeros(node_count), np.full(node_count, -0.25)])
    zero = np.zeros(2 * node_count)
    low, high = both / 2, (1 + both) / 2
    own = np.concatenate(
        [
            np.stack(angle_rows(low * turn, low**2 * turn, quarter)),
            np.stack(angle_rows(high * turn, high**2 * turn, quarter)),
        ],
        axis=1,
    )
    undo = np.stack(angle_rows(-both * turn, -(both**2) * turn, zero))
    undo_quarter = np.stack(angle_rows(-both * turn, -(both**2) * turn, quarter))
    wide = 2 * node_count
    out = np.zeros((LEVELS + 1, 2 * LANES, 2 * wide))
    for level in range(LEVELS):
        out[level, TILE * level : TILE * (level + 1)] = own
        if level:
            at = HALF + TILE * (level - 1)
            out[level, at : at + TILE, :wide] = undo
            at = LANES + TILE * (level - 1)
            out[level, at : at + TILE, wide:] = undo
    at = TILE * (LEVELS - 1)
    out[LEVELS, at : at + TILE, :wide] = undo_quarter
    out[LEVELS, HALF + at : HALF + at + TILE, wide:] = undo_quarter
    return out.astype(ml_dtypes.bfloat16)


def cos_turns(t):
    r = t - ((t + MAGIC) - MAGIC)
    w = 0.25 - jnp.abs(r)
    z = w * w
    p = z * C3 + C2
    p = p * z + C1
    p = p * z + C0
    return p * w


def _fit():
    w = np.cos(np.pi * (np.arange(400) + 0.5) / 800) * 0.25
    z = w * w
    target = np.sin(2 * np.pi * w) / w
    basis = np.stack([z**n for n in range(4)], 1)
    return [float(c) for c in np.linalg.lstsq(basis * w[:, None], target * w, rcond=None)[0]]


C0, C1, C2, C3 = _fit()


def kernel(rows, lane, step, got_ref, rates_ref, mats_ref, angle_ref, out_ref, turns_ref, state_a, state_b):
    levels = LEVELS
    wide_rows = 2 * rows
    row_id = lax.broadcasted_iota(jnp.int32, (TILE, wide_rows), 0)
    even = row_id % 2 == 0
    left_half = lax.broadcasted_iota(jnp.int32, (wide_rows, LANES), 1) < HALF

    def rate(m, level, kind):
        at = 4 * level + 2 * kind
        return jnp.concatenate(
            [rates_ref[m, at + c : at + c + 1, lane : lane + rows] for c in range(2)], 1
        )

    def make_turns(m, carry):
        tiles = []
        for level in range(levels):
            a, q = (jnp.broadcast_to(rate(m, level, kind), even.shape) for kind in range(2))
            base = jnp.where(even, a, q)
            first = base.astype(BF).astype(F32)
            rest = base - first
            second = rest.astype(BF).astype(F32)
            third = rest - second
            tile = jnp.where(row_id < 6, first, jnp.where(row_id < 10, second, third))
            tiles.append(jnp.where(row_id < 12, tile, jnp.where(row_id == 12, 1.0, 0.0)))
        turns_ref[m] = jnp.concatenate([*tiles, *tiles], 0).T.astype(BF)
        return carry

    lax.fori_loop(0, GROUP, make_turns, 0, unroll=2)

    def angles(firsts, seconds, thirds, stage):
        if not seconds:
            held = jnp.concatenate(firsts, 0)
        else:
            held = jnp.concatenate(
                [jnp.where(left_half, f, s) for f, s in zip(firsts, seconds)], 0
            )
        if not thirds:
            return jnp.dot(held, angle_ref[stage, :LANES], preferred_element_type=F32)
        held = jnp.concatenate([held, jnp.concatenate(thirds, 0)], 1)
        return jnp.dot(held, angle_ref[stage], preferred_element_type=F32)

    def combine(sources, turns, stage):
        phases = cos_turns(turns)
        highs, lows = [], []
        for n, pairs in enumerate(sources):
            high, low = [], []
            for s, (x, ix) in enumerate(pairs):
                phase = phases[n * wide_rows : (n + 1) * wide_rows, s * LANES : (s + 1) * LANES]
                turned = pltpu.roll(phase, HALF, 1)
                moved = x * jnp.where(left_half, phase, turned) + ix * jnp.where(left_half, turned, phase)
                top = moved.astype(BF)
                high.append(top)
                low.append((moved - top.astype(F32)).astype(BF))
            highs.append(jnp.concatenate(high, 1))
            lows.append(jnp.concatenate(low, 1))
        wide = jnp.dot(jnp.concatenate(highs, 0), mats_ref[stage], preferred_element_type=F32)
        narrow = jnp.dot(
            jnp.concatenate(lows, 0), mats_ref[stage, :, :LANES], preferred_element_type=F32
        )
        return wide[:, :LANES] + wide[:, LANES:] + narrow

    def times_i(x):
        other = pltpu.roll(x, HALF, 1)
        return jnp.where(left_half[: x.shape[0]], -other, other)

    def twice(x):
        return jnp.concatenate([x, x], 0)

    def level_stage(level, source, write):
        bit = levels - 1 - level

        def half_at(e):
            return pl.ds(pl.multiple_of(e * rows, rows), rows)

        def read(k, e):
            return source[k, half_at(e), :]

        def body(n, carry):
            sources, first, second, third, units = [], [], [], [], []
            for j in range(step):
                m = n * step + j
                e = (m >> (bit + 1)) & 1
                k1 = m | (2 << bit)
                k0 = k1 - (2 << bit)
                x0, x1 = read(k0, e), read(k1, e)
                sources.append(((twice(x0), twice(times_i(x0))), (twice(x1), twice(times_i(x1)))))
                if level:
                    second.append(twice(turns_ref[k0, half_at(e), :]))
                    third.append(twice(turns_ref[k1, half_at(e), :]))
                first.append(turns_ref[m])
                units.append(m)
            u = combine(sources, angles(first, second, third, level), level)
            for j, m in enumerate(units):
                write[m] = u[j * wide_rows : (j + 1) * wide_rows]
            return carry

        lax.fori_loop(0, GROUP // step, body, 0, unroll=UNROLL)

    level_stage(0, got_ref, state_a)
    level_stage(1, state_a, state_b)
    level_stage(2, state_b, state_a)
    level_stage(3, state_a, state_b)

    def last(n, carry):
        sources, first, second = [], [], []
        for j in range(step):
            i = n * step + j
            x0, x1 = state_b[2 * i], state_b[2 * i + 1]
            sources.append(((x0, times_i(x0)), (x1, times_i(x1))))
            first.append(turns_ref[2 * i])
            second.append(turns_ref[2 * i + 1])
        u = combine(sources, angles(first, second, [], levels), levels)
        for j in range(2 * step):
            out_ref[n * (2 * step) + j] = u[j * rows : (j + 1) * rows]
        return carry

    lax.fori_loop(0, GROUP // (2 * step), last, 0, unroll=UNROLL)


def finish(rows, step, got_ref, rates_ref, mats_ref, angle_ref, before_ref, out_ref, image, turns_ref, state_a, state_b, sems):
    ahead = before_ref.shape[1]
    held = pltpu.make_async_copy(before_ref, out_ref.at[:, pl.ds(0, ahead), :], sems.at[0])
    held.start()
    kernel(rows, ahead, step, got_ref, rates_ref, mats_ref, angle_ref, image, turns_ref, state_a, state_b)
    mine = pltpu.make_async_copy(image, out_ref.at[:, pl.ds(ahead, rows), :], sems.at[1])
    mine.start()
    mine.wait()
    held.wait()


def butterfly(got, rates, mats, angle, rows, step, before=None):
    whole = pl.BlockSpec(memory_space=pltpu.VMEM)
    in_specs = [whole] * 4
    scratch = [
        pltpu.VMEM((GROUP, 2 * rows, LANES), BF),
        pltpu.VMEM((GROUP, 2 * rows, LANES), F32),
        pltpu.VMEM((GROUP, 2 * rows, LANES), F32),
    ]
    cost = pl.CostEstimate(
        flops=GROUP * rows * 9 * 2 * 512 * 128, bytes_accessed=GROUP * rows * 9 * LANES * 4, transcendentals=0
    )
    params = pltpu.CompilerParams(vmem_limit_bytes=32 << 20)
    if before is None:
        return pl.pallas_call(
            functools.partial(kernel, rows, 0, step),
            out_shape=jax.ShapeDtypeStruct((GROUP, rows, LANES), F32),
            in_specs=in_specs,
            out_specs=whole,
            scratch_shapes=scratch,
            compiler_params=params,
            cost_estimate=cost,
        )(got, rates, mats, angle)
    return pl.pallas_call(
        functools.partial(finish, rows, step),
        out_shape=jax.ShapeDtypeStruct((GROUP, before.shape[1] + rows, LANES), F32),
        in_specs=[*in_specs, pl.BlockSpec(memory_space=pl.ANY)],
        out_specs=pl.BlockSpec(memory_space=pl.ANY),
        scratch_shapes=[pltpu.VMEM((GROUP, rows, LANES), F32), *scratch, pltpu.SemaphoreType.DMA((2,))],
        compiler_params=params,
        cost_estimate=cost,
    )(got, rates, mats, angle, before)


def stage_matrices(translate, evaluate):
    zero = jnp.zeros_like(translate)
    levels = jnp.concatenate(
        [jnp.concatenate([translate, zero], -1), jnp.concatenate([zero, translate], -1)], axis=2
    ).reshape(LEVELS, -1, LANES)
    er, ei = evaluate[:, 0], evaluate[:, 1]
    last = jnp.concatenate(
        [jnp.concatenate([er, ei], -1), jnp.concatenate([-ei, er], -1)], axis=1
    ).reshape(1, -1, LANES)
    whole = jnp.concatenate([levels, last], 0)
    high = lax.reduce_precision(whole, 8, 7)
    return jnp.concatenate([high, whole - high], -1).astype(BF)


def per_device(weights, rates, translate, evaluate):
    half = weights.shape[1] // 2
    axes = ("y", "zl", "band")
    other = lax.ppermute(evaluate[0], "band", [(0, 1), (1, 0)])
    mine = lax.axis_index("band")
    halves = weights[0].reshape(2, GROUP, SLICE, LANES)
    phase_rates = rates[0].reshape(16, GROUP, SLICE).transpose(1, 0, 2)

    def exchange(x):
        return lax.all_to_all(x, axes, 0, 0, tiled=True)

    block = jnp.concatenate([halves[0, :, :FIRST], halves[1, :, :FIRST], phase_rates], axis=1)
    block, other = lax.optimization_barrier((block, other))
    got = exchange(block)
    both = jnp.stack(
        [jnp.where(mine == 0, evaluate[0], other), jnp.where(mine == 0, other, evaluate[0])]
    )
    mats = stage_matrices(translate, both)
    angle = jnp.asarray(angle_matrix(LANES // 2))
    rest = jnp.concatenate([halves[0, :, FIRST:], halves[1, :, FIRST:]], axis=1)
    turns = got[:, 2 * FIRST :]
    rest, turns = lax.optimization_barrier((rest, turns))
    got_rest = exchange(rest)
    image = butterfly(got, turns, mats, angle, FIRST, STEPS[0])
    image = butterfly(got_rest, turns, mats, angle, SLICE - FIRST, STEPS[1], image)
    return exchange(image).reshape(half, LANES)


def solution(mesh):
    fine = Mesh(mesh.devices.reshape(4, 4, 4, 2, 2), ("y", "zl", "x", "core", "band"))
    leaf = ("y", "zl", "x", "core")
    return jax.shard_map(
        per_device,
        mesh=fine,
        in_specs=(P("band", leaf, None), P("band", None, None, leaf), P(), P("band", None, None, None)),
        out_specs=P((*leaf, "band"), None),
        check_vma=False,
    )
```

```python
import functools

import jax
import jax.numpy as jnp
import ml_dtypes
import numpy as np
from jax import lax
from jax.experimental import pallas as pl
from jax.experimental.pallas import tpu as pltpu
from jax.sharding import Mesh, PartitionSpec as P

BF = jnp.bfloat16
F32 = jnp.float32
LANES = 128
GROUP = 32
TILE = 16
MAGIC = 12582912.0
LEVELS = 4
FAR = pl.ANY
PIECES = 8
HALF = 64
SLICE = 128
FIRST = 96
STEPS = (4, 16)
UNROLL = 4


def split3(values):
    parts = []
    rest = values.astype(np.float64)
    for _ in range(3):
        part = rest.astype(ml_dtypes.bfloat16).astype(np.float64)
        parts.append(part)
        rest = rest - part
    return parts


def angle_rows(linear, square, offset):
    l1, l2, l3 = split3(linear)
    s1, s2, s3 = split3(square)
    zero = np.zeros_like(linear)
    return [l1, s1, l2, s2, l3, s3, l1, s1, l2, s2, l1, s1, offset, zero, zero, zero]


def angle_matrix(node_count):
    ticks = np.arange(node_count, dtype=np.float64)
    nodes = 0.5 * (1.0 - np.cos(np.pi * (ticks + 0.5) / node_count))
    both = np.concatenate([nodes, nodes])
    turn = 1.0 / (2.0 * np.pi)
    quarter = np.concatenate([np.zeros(node_count), np.full(node_count, -0.25)])
    zero = np.zeros(2 * node_count)
    low, high = both / 2, (1 + both) / 2
    own = np.concatenate(
        [
            np.stack(angle_rows(low * turn, low**2 * turn, quarter)),
            np.stack(angle_rows(high * turn, high**2 * turn, quarter)),
        ],
        axis=1,
    )
    undo = np.stack(angle_rows(-both * turn, -(both**2) * turn, zero))
    undo_quarter = np.stack(angle_rows(-both * turn, -(both**2) * turn, quarter))
    wide = 2 * node_count
    out = np.zeros((LEVELS + 1, 2 * LANES, 2 * wide))
    for level in range(LEVELS):
        out[level, TILE * level : TILE * (level + 1)] = own
        if level:
            at = HALF + TILE * (level - 1)
            out[level, at : at + TILE, :wide] = undo
            at = LANES + TILE * (level - 1)
            out[level, at : at + TILE, wide:] = undo
    at = TILE * (LEVELS - 1)
    out[LEVELS, at : at + TILE, :wide] = undo_quarter
    out[LEVELS, HALF + at : HALF + at + TILE, wide:] = undo_quarter
    return out.astype(ml_dtypes.bfloat16)


def cos_turns(t):
    r = t - ((t + MAGIC) - MAGIC)
    w = 0.25 - jnp.abs(r)
    z = w * w
    p = z * C3 + C2
    p = p * z + C1
    p = p * z + C0
    return p * w


def _fit():
    w = np.cos(np.pi * (np.arange(400) + 0.5) / 800) * 0.25
    z = w * w
    target = np.sin(2 * np.pi * w) / w
    basis = np.stack([z**n for n in range(4)], 1)
    return [float(c) for c in np.linalg.lstsq(basis * w[:, None], target * w, rcond=None)[0]]


C0, C1, C2, C3 = _fit()


def kernel(rows, lane, step, operands, rates_ref, mats_ref, angle_ref, out_ref, turns_ref, state_a, state_b):
    levels = LEVELS
    wide_rows = 2 * rows
    row_id = lax.broadcasted_iota(jnp.int32, (TILE, wide_rows), 0)
    even = row_id % 2 == 0
    left_half = lax.broadcasted_iota(jnp.int32, (wide_rows, LANES), 1) < HALF

    def rate(m, level, kind):
        at = 4 * level + 2 * kind
        return jnp.concatenate(
            [rates_ref[m, at + c : at + c + 1, lane : lane + rows] for c in range(2)], 1
        )

    def make_turns(m, carry):
        tiles = []
        for level in range(levels):
            a, q = (jnp.broadcast_to(rate(m, level, kind), even.shape) for kind in range(2))
            base = jnp.where(even, a, q)
            first = base.astype(BF).astype(F32)
            rest = base - first
            second = rest.astype(BF).astype(F32)
            third = rest - second
            tile = jnp.where(row_id < 6, first, jnp.where(row_id < 10, second, third))
            tiles.append(jnp.where(row_id < 12, tile, jnp.where(row_id == 12, 1.0, 0.0)))
        turns_ref[m] = jnp.concatenate([*tiles, *tiles], 0).T.astype(BF)
        return carry

    lax.fori_loop(0, GROUP, make_turns, 0, unroll=2)
    for dma in operands:
        dma.wait()

    def angles(firsts, seconds, thirds, stage):
        if not seconds:
            held = jnp.concatenate(firsts, 0)
        else:
            held = jnp.concatenate(
                [jnp.where(left_half, f, s) for f, s in zip(firsts, seconds)], 0
            )
        if not thirds:
            return jnp.dot(held, angle_ref[stage, :LANES], preferred_element_type=F32)
        held = jnp.concatenate([held, jnp.concatenate(thirds, 0)], 1)
        return jnp.dot(held, angle_ref[stage], preferred_element_type=F32)

    def combine(sources, turns, stage):
        phases = cos_turns(turns)
        highs, lows = [], []
        for n, pairs in enumerate(sources):
            high, low = [], []
            for s, (x, ix) in enumerate(pairs):
                phase = phases[n * wide_rows : (n + 1) * wide_rows, s * LANES : (s + 1) * LANES]
                turned = pltpu.roll(phase, HALF, 1)
                moved = x * jnp.where(left_half, phase, turned) + ix * jnp.where(left_half, turned, phase)
                top = moved.astype(BF)
                high.append(top)
                low.append((moved - top.astype(F32)).astype(BF))
            highs.append(jnp.concatenate(high, 1))
            lows.append(jnp.concatenate(low, 1))
        wide = jnp.dot(jnp.concatenate(highs, 0), mats_ref[stage], preferred_element_type=F32)
        narrow = jnp.dot(
            jnp.concatenate(lows, 0), mats_ref[stage, :, :LANES], preferred_element_type=F32
        )
        return wide[:, :LANES] + wide[:, LANES:] + narrow

    def times_i(x):
        other = pltpu.roll(x, HALF, 1)
        return jnp.where(left_half[: x.shape[0]], -other, other)

    def twice(x):
        return jnp.concatenate([x, x], 0)

    def level_stage(level, source, write):
        bit = levels - 1 - level

        def half_at(e):
            return pl.ds(pl.multiple_of(e * rows, rows), rows)

        def read(k, e):
            return source[k, half_at(e), :]

        def body(n, carry):
            sources, first, second, third, units = [], [], [], [], []
            for j in range(step):
                m = n * step + j
                e = (m >> (bit + 1)) & 1
                k1 = m | (2 << bit)
                k0 = k1 - (2 << bit)
                x0, x1 = read(k0, e), read(k1, e)
                sources.append(((twice(x0), twice(times_i(x0))), (twice(x1), twice(times_i(x1)))))
                if level:
                    second.append(twice(turns_ref[k0, half_at(e), :]))
                    third.append(twice(turns_ref[k1, half_at(e), :]))
                first.append(turns_ref[m])
                units.append(m)
            u = combine(sources, angles(first, second, third, level), level)
            for j, m in enumerate(units):
                write[m] = u[j * wide_rows : (j + 1) * wide_rows]
            return carry

        lax.fori_loop(0, GROUP // step, body, 0, unroll=min(UNROLL, GROUP // step))

    level_stage(0, state_b, state_a)
    level_stage(1, state_a, state_b)
    level_stage(2, state_b, state_a)
    level_stage(3, state_a, state_b)

    def last(n, carry):
        sources, first, second = [], [], []
        for j in range(step):
            i = n * step + j
            x0, x1 = state_b[2 * i], state_b[2 * i + 1]
            sources.append(((x0, times_i(x0)), (x1, times_i(x1))))
            first.append(turns_ref[2 * i])
            second.append(turns_ref[2 * i + 1])
        u = combine(sources, angles(first, second, [], levels), levels)
        for j in range(2 * step):
            out_ref[n * (2 * step) + j] = u[j * rows : (j + 1) * rows]
        return carry

    lax.fori_loop(0, GROUP // (2 * step), last, 0, unroll=min(UNROLL, max(1, GROUP // (2 * step))))


def part(lane, rows, step, got_ref, first_ref, mats_far, angle_far, out_ref, image, rates, mats_ref, angle_ref, turns_ref, state_a, state_b, sems):
    turns = pltpu.make_async_copy(first_ref.at[:, pl.ds(first_ref.shape[1] - 16, 16), :], rates, sems.at[0])
    boxes = pltpu.make_async_copy(got_ref.at[:, pl.ds(0, 2 * rows), :], state_b, sems.at[1])
    angle = pltpu.make_async_copy(angle_far, angle_ref, sems.at[2])
    mats = pltpu.make_async_copy(mats_far, mats_ref, sems.at[3])
    for dma in (turns, boxes, angle, mats):
        dma.start()
    turns.wait()
    kernel(rows, lane, step, (boxes, angle, mats), rates, mats_ref, angle_ref, image, turns_ref, state_a, state_b)
    mine = pltpu.make_async_copy(image, out_ref.at[:, pl.ds(lane, rows), :], sems.at[4])
    mine.start()
    mine.wait()


def begin(rows, step, got_ref, mats_far, angle_far, out_ref, *scratch):
    part(0, rows, step, got_ref, got_ref, mats_far, angle_far, out_ref, *scratch)


def finish(lane, rows, step, got_ref, first_ref, mats_far, angle_far, before_ref, out_ref, *scratch):
    part(lane, rows, step, got_ref, first_ref, mats_far, angle_far, out_ref, *scratch)


def fill_message(rows, weights_ref, rates_ref, out_ref, held, sems):
    share = GROUP // PIECES
    arrive, leave = [], []
    for n in range(PIECES):
        at = pl.ds(n * share, share)
        for e in range(2):
            into = held.at[at, pl.ds(e * rows, rows), :]
            arrive.append(
                pltpu.make_async_copy(weights_ref.at[e, at, pl.ds(0, rows), :], into, sems.at[0, 2 * n + e])
            )
        leave.append(pltpu.make_async_copy(held.at[at], out_ref.at[at], sems.at[1, n]))
    for dma in arrive:
        dma.start()
    half = GROUP * LANES

    def move(p, carry):
        for level in range(LEVELS):
            for child in range(2):
                at = pl.ds(pl.multiple_of(child * half + p * LANES, LANES), LANES)
                for kind in range(2):
                    row = 2 * rows + 4 * level + 2 * kind + child
                    held[p, row : row + 1, :] = rates_ref[level, kind : kind + 1, at]
        return carry

    lax.fori_loop(0, GROUP, move, 0, unroll=4)
    for n in range(PIECES):
        arrive[2 * n].wait()
        arrive[2 * n + 1].wait()
        leave[n].start()
    for dma in leave:
        dma.wait()


def first_message(halves, rates):
    return pl.pallas_call(
        functools.partial(fill_message, FIRST),
        out_shape=jax.ShapeDtypeStruct((GROUP, 2 * FIRST + 16, LANES), F32),
        in_specs=[pl.BlockSpec(memory_space=FAR), pl.BlockSpec(memory_space=pltpu.VMEM)],
        out_specs=pl.BlockSpec(memory_space=FAR),
        scratch_shapes=[
            pltpu.VMEM((GROUP, 2 * FIRST + 16, LANES), F32),
            pltpu.SemaphoreType.DMA((2, 2 * PIECES)),
        ],
        cost_estimate=pl.CostEstimate(flops=0, bytes_accessed=8 << 20, transcendentals=0),
    )(halves, rates)


def butterfly(got, mats, angle, rows, step, first=None, before=None):
    far = pl.BlockSpec(memory_space=FAR)
    operands = [got, mats, angle] if before is None else [got, first, mats, angle, before]
    body = begin if before is None else functools.partial(finish, SLICE - rows)
    return pl.pallas_call(
        functools.partial(body, rows, step),
        out_shape=jax.ShapeDtypeStruct((GROUP, SLICE, LANES), F32),
        in_specs=[far] * len(operands),
        out_specs=far,
        scratch_shapes=[
            pltpu.VMEM((GROUP, rows, LANES), F32),
            pltpu.VMEM((GROUP, 16, LANES), F32),
            pltpu.VMEM(mats.shape, BF),
            pltpu.VMEM(angle.shape, BF),
            pltpu.VMEM((GROUP, 2 * rows, LANES), BF),
            pltpu.VMEM((GROUP, 2 * rows, LANES), F32),
            pltpu.VMEM((GROUP, 2 * rows, LANES), F32),
            pltpu.SemaphoreType.DMA((5,)),
        ],
        input_output_aliases={} if before is None else {4: 0},
        compiler_params=pltpu.CompilerParams(vmem_limit_bytes=60 << 20),
        cost_estimate=pl.CostEstimate(
            flops=GROUP * rows * 9 * 2 * 512 * 128,
            bytes_accessed=GROUP * rows * 9 * LANES * 4,
            transcendentals=0,
        ),
    )(*operands)


def stage_matrices(translate, evaluate):
    zero = jnp.zeros_like(translate)
    levels = jnp.concatenate(
        [jnp.concatenate([translate, zero], -1), jnp.concatenate([zero, translate], -1)], axis=2
    ).reshape(LEVELS, -1, LANES)
    er, ei = evaluate[:, 0], evaluate[:, 1]
    last = jnp.concatenate(
        [jnp.concatenate([er, ei], -1), jnp.concatenate([-ei, er], -1)], axis=1
    ).reshape(1, -1, LANES)
    whole = jnp.concatenate([levels, last], 0)
    high = lax.reduce_precision(whole, 8, 7)
    return jnp.concatenate([high, whole - high], -1).astype(BF)


def per_device(weights, rates, translate, evaluate):
    half = weights.shape[1] // 2
    axes = ("y", "zl", "band")
    other = lax.ppermute(evaluate[0], "band", [(0, 1), (1, 0)])
    mine = lax.axis_index("band")
    halves = weights[0].reshape(2, GROUP, SLICE, LANES)

    def exchange(x):
        return lax.all_to_all(x, axes, 0, 0, tiled=True)

    block, other = lax.optimization_barrier((first_message(halves, rates[0]), other))
    got = exchange(block)
    both = jnp.stack(
        [jnp.where(mine == 0, evaluate[0], other), jnp.where(mine == 0, other, evaluate[0])]
    )
    mats = stage_matrices(translate, both)
    angle = jnp.asarray(angle_matrix(LANES // 2))
    rest = jnp.concatenate([halves[0, :, FIRST:], halves[1, :, FIRST:]], axis=1)
    rest, mats = lax.optimization_barrier((rest, mats))
    got_rest = exchange(rest)
    image = butterfly(got, mats, angle, FIRST, STEPS[0])
    image = butterfly(got_rest, mats, angle, SLICE - FIRST, STEPS[1], got, image)
    return exchange(image).reshape(half, LANES)


def solution(mesh):
    fine = Mesh(mesh.devices.reshape(4, 4, 4, 2, 2), ("y", "zl", "x", "core", "band"))
    leaf = ("y", "zl", "x", "core")
    return jax.shard_map(
        per_device,
        mesh=fine,
        in_specs=(P("band", leaf, None), P("band", None, None, leaf), P(), P("band", None, None, None)),
        out_specs=P((*leaf, "band"), None),
        check_vma=False,
    )
```
